32 devices in a mesh: groups: 1, expert: 4 (over z), replica: 8 (over y, x, core).
Axes of the slice: x: 2, y: 2, z: 4, core: 2. Of those that a mesh axis runs over, the one named last changes fastest.
Arguments:
- beam_rows: bfloat16 [32, 4096], P(('groups', 'expert', 'replica')), may hold values from -6 to 6
- norm_gain: float32 [4096], replicated, may hold values from 0.1 to 1.9
- router: bfloat16 [4096, 4], replicated, may hold values from -0.09375 to 0.09375
- gate_proj: bfloat16 [4, 4096, 1024], P('expert', None, 'replica'), may hold values from -0.09375 to 0.09375
- up_proj: bfloat16 [4, 4096, 1024], P('expert', None, 'replica'), may hold values from -0.09375 to 0.09375
- down_proj: bfloat16 [4, 1024, 4096], P('expert', 'replica'), may hold values from -0.1875 to 0.1875
- routes: int32 [32, 2], P(('groups', 'expert')), may hold values from 0 to 3, all different within a row; in each aligned block of 8 rows (0 to 7, 8 to 15, ...) at most 8 rows name the same one
Outputs:
- expert_out: bfloat16 [32, 4096], P(('groups', 'expert', 'replica'))
The draws below stay inside these ranges and needn't reach their ends.
Inputs may be any that keep to these rules, and one draw needn't show every extreme that they name: `routes`: each row names 2 different experts. Among the 8 rows of one index of expert (rows k * 8 to (k + 1) * 8 - 1) at most 8 rows name one expert, and in some such block one expert is named by exactly 8 rows.
All inputs are finite; a program needn't handle non-finite values.
Results may differ from the reference program's by a relative error of at most 0.0057.
Values may be sent and summed in bfloat16 or wider, within the bound.
A program may use at most 64 MiB of HBM per device.

```python
import math
import jax
import jax.numpy as jnp
import numpy as np
from jax import lax

D = 4096
FF = 1024
EXPERTS = 4
TOP = 2
BLOCK = 8
ROWS = 32
CAP = 8


def levels(stream_key, dims, pieces, smallest, top_value):
    factor_of = 1.0
    for axis_at, shards_of in pieces:
        steps = jax.random.uniform(jax.random.fold_in(jax.random.fold_in(stream_key, 6), axis_at), (shards_of,), jnp.float32, smallest / len(pieces), top_value / len(pieces))
        factor_of = factor_of * jnp.repeat(jnp.exp(steps), dims[axis_at] // shards_of).reshape((-1,) + (1,) * (len(dims) - 1 - axis_at))
    return factor_of


def shared_out(stream_key, own, number, rows, amount, top, bound, lean):
    ranking = jax.random.permutation(stream_key, amount)
    heavy_load, ordinary = shares(amount, rows * top, bound, lean, True), shares(amount, rows * top, bound, lean, False)
    places = jnp.arange(amount)

    def named(lengths, turn):
        used = int((lengths > 0).sum())
        fixed = max(1, used // 4)
        moved = fixed + (places - fixed + turn * (used - fixed)) % max(1, amount - fixed)
        return jnp.zeros((amount,), jnp.int32).at[ranking[jnp.where(places < fixed, places, moved)]].set(jnp.asarray(lengths, jnp.int32))

    lengths = jnp.where(number % 4 == 0, named(heavy_load, number // 4), named(ordinary, number - number // 4 - 1))
    mixed = jax.random.permutation(jax.random.fold_in(own, 3), amount)
    giver, receiver = mixed[0:amount // 2 * 2:2], mixed[1:amount // 2 * 2:2]
    margin = jnp.minimum(lengths[giver] - 1, bound - lengths[receiver]) // 2
    margin = jnp.where((giver == ranking[0]) | (receiver == ranking[0]) | (lengths[receiver] == 0), 0, jnp.maximum(margin, 0))
    moved = jax.random.randint(jax.random.fold_in(own, 4), (amount // 2,), 0, 1 << 20) % (margin + 1)
    lengths = lengths.at[giver].add(-moved).at[receiver].add(moved)
    labels = jnp.searchsorted(jnp.cumsum(lengths), jnp.arange(rows * top), side="right").astype(jnp.int32)
    listing = labels.reshape(top, rows).T
    listing = listing[jax.random.permutation(jax.random.fold_in(own, 1), rows)]
    turn = jax.random.randint(jax.random.fold_in(own, 2), (rows, 1), 0, top)
    return jnp.take_along_axis(listing, (jnp.arange(top)[None, :] + turn) % top, axis=1)


def shares(amount, total, limit, lean, full):
    loads = [(1 << 20) // math.isqrt(standing ** lean) + 1 for standing in range(1, amount + 1)]
    largest = limit if full else min(limit, max(-(-total // amount), total * loads[0] // sum(loads)))
    least = 1 if total - largest >= amount - 1 else 0
    counts, spare = [largest] + [least] * (amount - 1), total - largest - least * (amount - 1)
    while spare > 0:
        free = [i for i in range(1, amount) if counts[i] < largest] or [i for i in range(1, amount) if counts[i] < limit]
        mass, left = sum([loads[i] for i in free]), spare
        for i in free:
            more = min(limit - counts[i], max(1, left * loads[i] // mass), spare)
            counts[i] = counts[i] + more
            spare = spare - more
    return np.array(counts)


def gaussian(own_key, shape, scale, bound, shards=(), held_as=jnp.bfloat16):
    array = jax.random.normal(own_key, shape, jnp.float32) * scale
    if len(shards) > 0:
        array = levels(own_key, shape, shards, -0.22, 0.18) * array
    return jnp.clip(array, min=-bound, max=bound).astype(held_as)


def setup_inputs(seed: int = 0, part: int = 0) -> dict:
    arg_keys = jax.random.split(jax.random.key(seed), 8)
    part_keys = jax.random.split(jax.random.fold_in(arg_keys[7], part), 8)
    beam_rows = gaussian(part_keys[0], (ROWS, D), 1.0, 6.0, ((0, 32),))
    norm_gain = jnp.clip(1.0 + 0.18 * jax.random.normal(arg_keys[1], (D,), jnp.float32), 0.1, 1.9)
    router = gaussian(arg_keys[2], (D, EXPERTS), D ** -0.5, 0.09375)
    gate_proj = gaussian(arg_keys[3], (EXPERTS, D, FF), D ** -0.5, 0.09375, ((0, 4), (2, 8)))
    up_proj = gaussian(arg_keys[4], (EXPERTS, D, FF), D ** -0.5, 0.09375, ((0, 4), (2, 8)))
    down_proj = gaussian(arg_keys[5], (EXPERTS, FF, D), FF ** -0.5, 0.1875, ((0, 4), (1, 8)))
    routes_keys = jax.random.split(jax.random.fold_in(part_keys[6], 1), ROWS // BLOCK)
    routes_turns = jax.random.permutation(jax.random.fold_in(part_keys[6], 3), ROWS // BLOCK)
    routes = jax.vmap(lambda own, number: shared_out(jax.random.fold_in(part_keys[6], 2), own, number, BLOCK, EXPERTS, TOP, CAP, 2))(routes_keys, routes_turns).reshape((ROWS, TOP))
    return dict(beam_rows=beam_rows, norm_gain=norm_gain, router=router, gate_proj=gate_proj, up_proj=up_proj, down_proj=down_proj, routes=routes)


ROUTE_SCALE = 2.5

def rms_rows(beam_rows, norm_gain):
    values = beam_rows.astype(jnp.float32)
    inverse_rms = lax.rsqrt(lax.optimization_barrier(jnp.mean(values * values, axis=-1, keepdims=True)) + 1e-06)
    return (values * inverse_rms * norm_gain).astype(jnp.bfloat16)

def route_weights(normed, router, routes):
    expert_count = router.shape[1]
    logits = jnp.dot(normed, router, preferred_element_type=jnp.float32)
    members = lax.optimization_barrier(jnp.sum((routes[:, :, None] == jnp.arange(expert_count, dtype=jnp.int32)[None, None, :]).astype(jnp.float32), axis=1))
    chosen = jax.nn.sigmoid(logits) * members
    return (ROUTE_SCALE * chosen / lax.optimization_barrier(jnp.sum(chosen, axis=1, keepdims=True)), members)

def expert_part(normed, gate_slice, up_slice, down_slice):
    gate_act = jnp.dot(normed, gate_slice, preferred_element_type=jnp.float32)
    up_act = jnp.dot(normed, up_slice, preferred_element_type=jnp.float32)
    hidden = (jax.nn.silu(gate_act) * up_act).astype(jnp.bfloat16)
    return jnp.dot(hidden, down_slice, preferred_element_type=jnp.float32)

def reference(beam_rows, norm_gain, router, gate_proj, up_proj, down_proj, routes):
    normed = rms_rows(beam_rows, norm_gain)
    combine_weights, members = route_weights(normed, router, routes)

    def add_expert(running, packed):
        gate_slice, up_slice, down_slice, column = packed
        return (running + column[:, None] * expert_part(normed, gate_slice, up_slice, down_slice), None)
    empty_sums = jnp.zeros(beam_rows.shape, jnp.float32)
    moe, _ = lax.scan(add_expert, empty_sums, (gate_proj, up_proj, down_proj, combine_weights.T))
    return (beam_rows.astype(jnp.float32) + moe).astype(jnp.bfloat16)
```

```python
import functools

import jax
import jax.numpy as jnp
from jax import lax
from jax.experimental import pallas as pl
from jax.experimental.pallas import tpu as pltpu
from jax.sharding import PartitionSpec as P

ROUTE_SCALE = 2.5
LANES = 128


def moe_kernel(
    Z,
    R,
    x_ref,
    gain_ref,
    router_ref,
    routes_ref,
    gate_ref,
    up_ref,
    down_ref,
    out_ref,
    wgu,
    wd,
    xs,
    rows,
    flat,
    lhs,
    part,
    snd,
    got,
    acc,
    zsnd,
    zgot,
    wts,
    w_sem,
    ag_zsend,
    ag_zrecv,
    ag_psend,
    ag_precv,
    rs_psend,
    rs_precv,
    rs_zsend,
    rs_zrecv,
):
    C = xs.shape[0]
    F = wd.shape[0]
    M = Z * R
    z = lax.axis_index("expert")
    r = lax.axis_index("replica")
    z_peers = [(d, lax.rem(z + d, Z)) for d in range(1, Z)]
    r_peers = [(d, lax.rem(r + d, R)) for d in range(1, R)]

    barrier = pltpu.get_barrier_semaphore()
    for _, zp in z_peers:
        pl.semaphore_signal(
            barrier, inc=1, device_id={"expert": zp}, device_id_type=pl.DeviceIdType.MESH
        )
    for _, rp in r_peers:
        pl.semaphore_signal(
            barrier, inc=1, device_id={"replica": rp}, device_id_type=pl.DeviceIdType.MESH
        )

    weights = [
        pltpu.make_async_copy(gate_ref.at[0], wgu.at[:, pl.ds(0, F)], w_sem.at[0]),
        pltpu.make_async_copy(up_ref.at[0], wgu.at[:, pl.ds(F, F)], w_sem.at[1]),
        pltpu.make_async_copy(down_ref.at[0], wd, w_sem.at[2]),
    ]
    for copy in weights:
        copy.start()

    for c in range(C):
        xs[pl.ds(c, 1), :] = x_ref[:, pl.ds(c * LANES, LANES)].astype(jnp.float32)
    x = xs[...]
    squares = jnp.sum(jnp.sum(x * x, axis=0, keepdims=True), axis=1, keepdims=True)
    inverse_rms = lax.rsqrt(squares / (C * LANES) + 1e-06)
    normed = (x * inverse_rms * gain_ref[...]).astype(jnp.bfloat16)
    rows[r, z] = normed

    pl.semaphore_wait(barrier, (Z - 1) + (R - 1))

    def z_copy(d, zp, own):
        return pltpu.make_async_remote_copy(
            src_ref=rows.at[r, z],
            dst_ref=rows.at[r, z] if own else rows.at[r, zp],
            send_sem=ag_zsend.at[d],
            recv_sem=ag_zrecv.at[z] if own else ag_zrecv.at[zp],
            device_id={"expert": zp},
            device_id_type=pl.DeviceIdType.MESH,
        )

    def p_send(k, row_z, d, rp):
        return pltpu.make_async_remote_copy(
            src_ref=rows.at[r, row_z],
            dst_ref=rows.at[r, row_z],
            send_sem=ag_psend.at[k, d],
            recv_sem=ag_precv.at[row_z, r],
            device_id={"replica": rp},
            device_id_type=pl.DeviceIdType.MESH,
        )

    def p_recv(k, row_z, d, rp):
        return pltpu.make_async_remote_copy(
            src_ref=rows.at[rp, row_z],
            dst_ref=rows.at[rp, row_z],
            send_sem=ag_psend.at[k, d],
            recv_sem=ag_precv.at[row_z, rp],
            device_id={"replica": rp},
            device_id_type=pl.DeviceIdType.MESH,
        )

    for d, zp in z_peers:
        z_copy(d, zp, True).start()
    for d, rp in r_peers:
        p_send(0, z, d, rp).start()

    def spread(rr, zz):
        at = pl.multiple_of((rr * Z + zz) * C, C)
        flat[pl.ds(at, C), :] = rows[rr, zz].astype(jnp.float32)

    for d, zp in z_peers:
        z_copy(d, zp, False).wait_recv()
        for e, rp in r_peers:
            p_send(d, zp, e, rp).start()

    E = router_ref.shape[0]
    xs[...] = normed.astype(jnp.float32)
    logit_sums = jnp.zeros((E, LANES), jnp.float32)
    for c in range(C):
        logit_sums += (
            router_ref[:, pl.ds(c * LANES, LANES)].astype(jnp.float32) * xs[pl.ds(c, 1), :]
        )
    logits = jnp.broadcast_to(jnp.sum(logit_sums, axis=1, keepdims=True), (E, LANES))
    expert_ids = lax.broadcasted_iota(jnp.int32, (E, LANES), 0)
    members = jnp.zeros((E, LANES), jnp.float32)
    for t in range(routes_ref.shape[0]):
        members += (expert_ids == routes_ref[t, r]).astype(jnp.float32)
    chosen = members / (1.0 + jnp.exp(-logits))
    wts[...] = ROUTE_SCALE * chosen / jnp.sum(chosen, axis=0, keepdims=True)

    spread(r, z)
    for _, zp in z_peers:
        spread(r, zp)
    for k, zz in [(0, z)] + z_peers:
        for e, rp in r_peers:
            p_recv(k, zz, e, rp).wait_recv()
            spread(rp, zz)
    for c in range(C):
        lhs[:, pl.ds(c * LANES, LANES)] = flat[pl.ds(c, M, stride=C), :].astype(jnp.bfloat16)

    weights[0].wait()
    weights[1].wait()
    gate_up = jnp.dot(lhs[...], wgu[...], preferred_element_type=jnp.float32)
    gate_act, up_act = gate_up[:, :F], gate_up[:, F:]
    hidden = (gate_act / (1.0 + jnp.exp(-gate_act)) * up_act).astype(jnp.bfloat16)
    weights[2].wait()
    step = 4
    for n in range(C // step):
        piece = jnp.dot(
            hidden,
            wd[:, pl.ds(n * step * LANES, step * LANES)],
            preferred_element_type=jnp.float32,
        )
        for j in range(step):
            part[pl.ds(n * step + j, M, stride=C), :] = piece[:, j * LANES : (j + 1) * LANES]

    span = Z * C

    def rs_send(d, rp):
        return pltpu.make_async_remote_copy(
            src_ref=snd.at[rp],
            dst_ref=got.at[r],
            send_sem=rs_psend.at[d],
            recv_sem=rs_precv.at[r],
            device_id={"replica": rp},
            device_id_type=pl.DeviceIdType.MESH,
        )

    def rs_recv(d, rp):
        return pltpu.make_async_remote_copy(
            src_ref=snd.at[rp],
            dst_ref=got.at[rp],
            send_sem=rs_psend.at[d],
            recv_sem=rs_precv.at[rp],
            device_id={"replica": rp},
            device_id_type=pl.DeviceIdType.MESH,
        )

    for d, rp in r_peers:
        at = pl.multiple_of(rp * span, span)
        snd[rp] = part[pl.ds(at, span), :].astype(jnp.bfloat16)
        rs_send(d, rp).start()
    acc[...] = part[pl.ds(pl.multiple_of(r * span, span), span), :]
    for d, rp in r_peers:
        rs_recv(d, rp).wait_recv()
        acc[...] += got[rp].astype(jnp.float32)

    def rz_copy(d, zp, own):
        return pltpu.make_async_remote_copy(
            src_ref=zsnd.at[zp],
            dst_ref=zgot.at[z] if own else zgot.at[zp],
            send_sem=rs_zsend.at[d],
            recv_sem=rs_zrecv.at[z] if own else rs_zrecv.at[zp],
            device_id={"expert": zp},
            device_id_type=pl.DeviceIdType.MESH,
        )

    for d, zp in z_peers:
        zsnd[zp] = acc[pl.ds(pl.multiple_of(zp * C, C), C), :].astype(jnp.bfloat16)
        rz_copy(d, zp, True).start()
    total = acc[pl.ds(pl.multiple_of(z * C, C), C), :] * wts[pl.ds(z, 1), :]
    for d, zp in z_peers:
        rz_copy(d, zp, False).wait_recv()
        total += zgot[zp].astype(jnp.float32) * wts[pl.ds(zp, 1), :]

    for c in range(C):
        lane = pl.ds(c * LANES, LANES)
        out_ref[:, lane] = (
            x_ref[:, lane].astype(jnp.float32) + total[c : c + 1, :]
        ).astype(jnp.bfloat16)

    for d, zp in z_peers:
        z_copy(d, zp, True).wait_send()
        rz_copy(d, zp, True).wait_send()
        for e, rp in r_peers:
            p_send(d, zp, e, rp).wait_send()
    for d, rp in r_peers:
        p_send(0, z, d, rp).wait_send()
        rs_send(d, rp).wait_send()


def solution(mesh):
    Z, R = mesh.shape["expert"], mesh.shape["replica"]

    def on_device(beam_rows, norm_gain, router, gate_proj, up_proj, down_proj, routes):
        D = beam_rows.shape[1]
        F = gate_proj.shape[2]
        C = D // LANES
        M = Z * R
        E = router.shape[1]
        vmem = pl.BlockSpec(memory_space=pltpu.VMEM)
        smem = pl.BlockSpec(memory_space=pltpu.SMEM)
        anywhere = pl.BlockSpec(memory_space=pl.ANY)
        dma = pltpu.SemaphoreType.DMA
        return pl.pallas_call(
            functools.partial(moe_kernel, Z, R),
            out_shape=jax.ShapeDtypeStruct(beam_rows.shape, jnp.bfloat16),
            in_specs=[vmem, vmem, vmem, smem, anywhere, anywhere, anywhere],
            out_specs=vmem,
            scratch_shapes=[
                pltpu.VMEM((D, 2 * F), jnp.bfloat16),
                pltpu.VMEM((F, D), jnp.bfloat16),
                pltpu.VMEM((C, LANES), jnp.float32),
                pltpu.VMEM((R, Z, C, LANES), jnp.bfloat16),
                pltpu.VMEM((M * C, LANES), jnp.float32),
                pltpu.VMEM((M, D), jnp.bfloat16),
                pltpu.VMEM((M * C, LANES), jnp.float32),
                pltpu.VMEM((R, Z * C, LANES), jnp.bfloat16),
                pltpu.VMEM((R, Z * C, LANES), jnp.bfloat16),
                pltpu.VMEM((Z * C, LANES), jnp.float32),
                pltpu.VMEM((Z, C, LANES), jnp.bfloat16),
                pltpu.VMEM((Z, C, LANES), jnp.bfloat16),
                pltpu.VMEM((E, LANES), jnp.float32),
                dma((3,)),
                dma((Z,)),
                dma((Z,)),
                dma((Z, R)),
                dma((Z, R)),
                dma((R,)),
                dma((R,)),
                dma((Z,)),
                dma((Z,)),
            ],
            compiler_params=pltpu.CompilerParams(
                collective_id=0, has_side_effects=True, vmem_limit_bytes=50 * 2**20
            ),
        )(
            beam_rows,
            norm_gain.reshape(C, LANES),
            router.T,
            routes.T,
            gate_proj,
            up_proj,
            down_proj,
        )

    placed = (
        P(("groups", "expert", "replica"), None),
        P(),
        P(),
        P("expert", None, "replica"),
        P("expert", None, "replica"),
        P("expert", "replica", None),
        P(("groups", "expert"), None),
    )
    return jax.shard_map(
        on_device,
        mesh=mesh,
        in_specs=placed,
        out_specs=P(("groups", "expert", "replica"), None),
        check_vma=False,
    )
```

```python
import functools

import jax
import jax.numpy as jnp
from jax import lax
from jax.experimental import pallas as pl
from jax.experimental.pallas import tpu as pltpu
from jax.sharding import PartitionSpec as P

ROUTE_SCALE = 2.5
LANES = 128
VMEM_BYTES = 63 * 2**20


def moe_kernel(
    Z,
    R,
    x_hbm,
    gain_hbm,
    router_hbm,
    routes_hbm,
    gate_ref,
    up_ref,
    down_ref,
    out_ref,
    x_ref,
    gain_ref,
    router_ref,
    routes_ref,
    wgu,
    wd,
    xs,
    rows,
    flat,
    lhs,
    part,
    snd,
    got,
    acc,
    zsnd,
    zgot,
    wts,
    w_sem,
    ag_zsend,
    ag_zrecv,
    ag_psend,
    ag_precv,
    rs_psend,
    rs_precv,
    rs_zsend,
    rs_zrecv,
):
    C = xs.shape[0]
    F = wd.shape[0]
    M = Z * R
    z = lax.axis_index("expert")
    r = lax.axis_index("replica")
    z_peers = [(d, lax.rem(z + d, Z)) for d in range(1, Z)]
    r_peers = [(d, lax.rem(r + d, R)) for d in range(1, R)]

    small = [
        pltpu.make_async_copy(x_hbm, x_ref, w_sem.at[3]),
        pltpu.make_async_copy(gain_hbm, gain_ref, w_sem.at[4]),
        pltpu.make_async_copy(router_hbm, router_ref, w_sem.at[5]),
        pltpu.make_async_copy(routes_hbm, routes_ref, w_sem.at[6]),
    ]
    for copy in small:
        copy.start()

    barrier = pltpu.get_barrier_semaphore()
    for _, zp in z_peers:
        pl.semaphore_signal(
            barrier, inc=1, device_id={"expert": zp}, device_id_type=pl.DeviceIdType.MESH
        )
    for _, rp in r_peers:
        pl.semaphore_signal(
            barrier, inc=1, device_id={"replica": rp}, device_id_type=pl.DeviceIdType.MESH
        )

    weights = [
        pltpu.make_async_copy(gate_ref.at[0], wgu.at[:, pl.ds(0, F)], w_sem.at[0]),
        pltpu.make_async_copy(up_ref.at[0], wgu.at[:, pl.ds(F, F)], w_sem.at[1]),
        pltpu.make_async_copy(down_ref.at[0], wd, w_sem.at[2]),
    ]
    for copy in weights:
        copy.start()

    small[0].wait()
    small[1].wait()
    for c in range(C):
        xs[pl.ds(c, 1), :] = x_ref[:, pl.ds(c * LANES, LANES)].astype(jnp.float32)
    x = xs[...]
    squares = jnp.sum(jnp.sum(x * x, axis=0, keepdims=True), axis=1, keepdims=True)
    inverse_rms = lax.rsqrt(squares / (C * LANES) + 1e-06)
    normed = (x * inverse_rms * gain_ref[...]).astype(jnp.bfloat16)
    rows[r, z] = normed

    pl.semaphore_wait(barrier, (Z - 1) + (R - 1))

    def z_copy(d, zp, own):
        return pltpu.make_async_remote_copy(
            src_ref=rows.at[r, z],
            dst_ref=rows.at[r, z] if own else rows.at[r, zp],
            send_sem=ag_zsend.at[d],
            recv_sem=ag_zrecv.at[z] if own else ag_zrecv.at[zp],
            device_id={"expert": zp},
            device_id_type=pl.DeviceIdType.MESH,
        )

    def p_send(k, row_z, d, rp):
        return pltpu.make_async_remote_copy(
            src_ref=rows.at[r, row_z],
            dst_ref=rows.at[r, row_z],
            send_sem=ag_psend.at[k, d],
            recv_sem=ag_precv.at[row_z, r],
            device_id={"replica": rp},
            device_id_type=pl.DeviceIdType.MESH,
        )

    def p_recv(k, row_z, d, rp):
        return pltpu.make_async_remote_copy(
            src_ref=rows.at[rp, row_z],
            dst_ref=rows.at[rp, row_z],
            send_sem=ag_psend.at[k, d],
            recv_sem=ag_precv.at[row_z, rp],
            device_id={"replica": rp},
            device_id_type=pl.DeviceIdType.MESH,
        )

    for d, zp in z_peers:
        z_copy(d, zp, True).start()
    for d, rp in r_peers:
        p_send(0, z, d, rp).start()

    def spread(rr, zz):
        at = pl.multiple_of((rr * Z + zz) * C, C)
        flat[pl.ds(at, C), :] = rows[rr, zz].astype(jnp.float32)

    for d, zp in z_peers:
        z_copy(d, zp, False).wait_recv()
        for e, rp in r_peers:
            p_send(d, zp, e, rp).start()

    small[2].wait()
    small[3].wait()
    E = router_ref.shape[0]
    xs[...] = normed.astype(jnp.float32)
    logit_sums = jnp.zeros((E, LANES), jnp.float32)
    for c in range(C):
        logit_sums += (
            router_ref[:, pl.ds(c * LANES, LANES)].astype(jnp.float32) * xs[pl.ds(c, 1), :]
        )
    logits = jnp.broadcast_to(jnp.sum(logit_sums, axis=1, keepdims=True), (E, LANES))
    expert_ids = lax.broadcasted_iota(jnp.int32, (E, LANES), 0)
    members = jnp.zeros((E, LANES), jnp.float32)
    for t in range(routes_ref.shape[0]):
        members += (expert_ids == routes_ref[t, r]).astype(jnp.float32)
    chosen = members / (1.0 + jnp.exp(-logits))
    wts[...] = ROUTE_SCALE * chosen / jnp.sum(chosen, axis=0, keepdims=True)

    spread(r, z)
    for _, zp in z_peers:
        spread(r, zp)
    for k, zz in [(0, z)] + z_peers:
        for e, rp in r_peers:
            p_recv(k, zz, e, rp).wait_recv()
            spread(rp, zz)
    for c in range(C):
        lhs[:, pl.ds(c * LANES, LANES)] = flat[pl.ds(c, M, stride=C), :].astype(jnp.bfloat16)

    weights[0].wait()
    weights[1].wait()
    gate_up = jnp.dot(lhs[...], wgu[...], preferred_element_type=jnp.float32)
    gate_act, up_act = gate_up[:, :F], gate_up[:, F:]
    hidden = (gate_act / (1.0 + jnp.exp(-gate_act)) * up_act).astype(jnp.bfloat16)
    weights[2].wait()
    step = 4
    for n in range(C // step):
        piece = jnp.dot(
            hidden,
            wd[:, pl.ds(n * step * LANES, step * LANES)],
            preferred_element_type=jnp.float32,
        )
        for j in range(step):
            part[pl.ds(n * step + j, M, stride=C), :] = piece[:, j * LANES : (j + 1) * LANES]

    span = Z * C

    def rs_send(d, rp):
        return pltpu.make_async_remote_copy(
            src_ref=snd.at[rp],
            dst_ref=got.at[r],
            send_sem=rs_psend.at[d],
            recv_sem=rs_precv.at[r],
            device_id={"replica": rp},
            device_id_type=pl.DeviceIdType.MESH,
        )

    def rs_recv(d, rp):
        return pltpu.make_async_remote_copy(
            src_ref=snd.at[rp],
            dst_ref=got.at[rp],
            send_sem=rs_psend.at[d],
            recv_sem=rs_precv.at[rp],
            device_id={"replica": rp},
            device_id_type=pl.DeviceIdType.MESH,
        )

    for d, rp in r_peers:
        at = pl.multiple_of(rp * span, span)
        snd[rp] = part[pl.ds(at, span), :].astype(jnp.bfloat16)
        rs_send(d, rp).start()
    acc[...] = part[pl.ds(pl.multiple_of(r * span, span), span), :]
    for d, rp in r_peers:
        rs_recv(d, rp).wait_recv()
        acc[...] += got[rp].astype(jnp.float32)

    def rz_copy(d, zp, own):
        return pltpu.make_async_remote_copy(
            src_ref=zsnd.at[zp],
            dst_ref=zgot.at[z] if own else zgot.at[zp],
            send_sem=rs_zsend.at[d],
            recv_sem=rs_zrecv.at[z] if own else rs_zrecv.at[zp],
            device_id={"expert": zp},
            device_id_type=pl.DeviceIdType.MESH,
        )

    for d, zp in z_peers:
        zsnd[zp] = acc[pl.ds(pl.multiple_of(zp * C, C), C), :].astype(jnp.bfloat16)
        rz_copy(d, zp, True).start()
    total = acc[pl.ds(pl.multiple_of(z * C, C), C), :] * wts[pl.ds(z, 1), :]
    for d, zp in z_peers:
        rz_copy(d, zp, False).wait_recv()
        total += zgot[zp].astype(jnp.float32) * wts[pl.ds(zp, 1), :]

    for c in range(C):
        lane = pl.ds(c * LANES, LANES)
        out_ref[:, lane] = (
            x_ref[:, lane].astype(jnp.float32) + total[c : c + 1, :]
        ).astype(jnp.bfloat16)

    for d, zp in z_peers:
        z_copy(d, zp, True).wait_send()
        rz_copy(d, zp, True).wait_send()
        for e, rp in r_peers:
            p_send(d, zp, e, rp).wait_send()
    for d, rp in r_peers:
        p_send(0, z, d, rp).wait_send()
        rs_send(d, rp).wait_send()


def solution(mesh):
    Z, R = mesh.shape["expert"], mesh.shape["replica"]

    def on_device(beam_rows, norm_gain, router, gate_proj, up_proj, down_proj, routes):
        D = beam_rows.shape[1]
        F = gate_proj.shape[2]
        C = D // LANES
        M = Z * R
        E = router.shape[1]
        vmem = pl.BlockSpec(memory_space=pltpu.VMEM)
        anywhere = pl.BlockSpec(memory_space=pl.ANY)
        dma = pltpu.SemaphoreType.DMA
        return pl.pallas_call(
            functools.partial(moe_kernel, Z, R),
            out_shape=jax.ShapeDtypeStruct(beam_rows.shape, jnp.bfloat16),
            in_specs=[anywhere] * 7,
            out_specs=vmem,
            scratch_shapes=[
                pltpu.VMEM(beam_rows.shape, beam_rows.dtype),
                pltpu.VMEM((C, LANES), jnp.float32),
                pltpu.VMEM((E, D), router.dtype),
                pltpu.SMEM(routes.shape[::-1], jnp.int32),
                pltpu.VMEM((D, 2 * F), jnp.bfloat16),
                pltpu.VMEM((F, D), jnp.bfloat16),
                pltpu.VMEM((C, LANES), jnp.float32),
                pltpu.VMEM((R, Z, C, LANES), jnp.bfloat16),
                pltpu.VMEM((M * C, LANES), jnp.float32),
                pltpu.VMEM((M, D), jnp.bfloat16),
                pltpu.VMEM((M * C, LANES), jnp.float32),
                pltpu.VMEM((R, Z * C, LANES), jnp.bfloat16),
                pltpu.VMEM((R, Z * C, LANES), jnp.bfloat16),
                pltpu.VMEM((Z * C, LANES), jnp.float32),
                pltpu.VMEM((Z, C, LANES), jnp.bfloat16),
                pltpu.VMEM((Z, C, LANES), jnp.bfloat16),
                pltpu.VMEM((E, LANES), jnp.float32),
                dma((7,)),
                dma((Z,)),
                dma((Z,)),
                dma((Z, R)),
                dma((Z, R)),
                dma((R,)),
                dma((R,)),
                dma((Z,)),
                dma((Z,)),
            ],
            compiler_params=pltpu.CompilerParams(
                collective_id=0, has_side_effects=True, vmem_limit_bytes=VMEM_BYTES
            ),
        )(
            beam_rows,
            norm_gain.reshape(C, LANES),
            router.T,
            routes.T,
            gate_proj,
            up_proj,
            down_proj,
        )

    placed = (
        P(("groups", "expert", "replica"), None),
        P(),
        P(),
        P("expert", None, "replica"),
        P("expert", None, "replica"),
        P("expert", "replica", None),
        P(("groups", "expert"), None),
    )
    return jax.shard_map(
        on_device,
        mesh=mesh,
        in_specs=placed,
        out_specs=P(("groups", "expert", "replica"), None),
        check_vma=False,
    )
```

```python
import functools

import jax
import jax.numpy as jnp
from jax import lax
from jax.experimental import pallas as pl
from jax.experimental.pallas import tpu as pltpu
from jax.sharding import PartitionSpec as P

ROUTE_SCALE = 2.5
LANES = 128
VMEM_BYTES = 63 * 2**20


def moe_kernel(
    Z,
    R,
    x_hbm,
    gain_hbm,
    router_hbm,
    routes_hbm,
    gate_ref,
    up_ref,
    down_ref,
    out_ref,
    x_ref,
    gain_ref,
    router_ref,
    routes_ref,
    wgu,
    wd,
    xs,
    rows,
    flat,
    lhs,
    part,
    psnd,
    pgot,
    acc,
    snd,
    got,
    wts,
    w_sem,
    ag_send,
    ag_pass,
    ag_recv,
    rs_psend,
    rs_precv,
    rs_send,
    rs_recv,
):
    C = xs.shape[0]
    F = wd.shape[0]
    M = Z * R
    z = lax.axis_index("expert")
    r = lax.axis_index("replica")
    core = lax.rem(r, 2)
    partner = r + 1 - 2 * core
    MESH = pl.DeviceIdType.MESH

    def flip(value, mask):
        bit = 1
        while bit <= mask:
            if mask & bit:
                value = value + bit - 2 * bit * lax.rem(lax.div(value, bit), 2)
            bit *= 2
        return value

    pairs = [(a, 2 * b) for a in range(Z) for b in range(R // 2) if a or b]
    pairs.sort(key=lambda p: p[0] + bin(p[1]).count("1"))
    peers = [(i, flip(z, a), flip(r, b)) for i, (a, b) in enumerate(pairs)]

    small = [
        pltpu.make_async_copy(x_hbm, x_ref, w_sem.at[3]),
        pltpu.make_async_copy(gain_hbm, gain_ref, w_sem.at[4]),
        pltpu.make_async_copy(router_hbm, router_ref, w_sem.at[5]),
        pltpu.make_async_copy(routes_hbm, routes_ref, w_sem.at[6]),
    ]
    for copy in small:
        copy.start()

    barrier = pltpu.get_barrier_semaphore()
    pl.semaphore_signal(barrier, inc=1, device_id={"replica": partner}, device_id_type=MESH)
    for _, zp, rp in peers:
        pl.semaphore_signal(
            barrier, inc=1, device_id={"expert": zp, "replica": rp}, device_id_type=MESH
        )

    weights = [
        pltpu.make_async_copy(gate_ref.at[0], wgu.at[:, pl.ds(0, F)], w_sem.at[0]),
        pltpu.make_async_copy(up_ref.at[0], wgu.at[:, pl.ds(F, F)], w_sem.at[1]),
        pltpu.make_async_copy(down_ref.at[0], wd, w_sem.at[2]),
    ]
    for copy in weights:
        copy.start()

    small[0].wait()
    small[1].wait()
    for c in range(C):
        xs[pl.ds(c, 1), :] = x_ref[:, pl.ds(c * LANES, LANES)].astype(jnp.float32)
    x = xs[...]
    squares = jnp.sum(jnp.sum(x * x, axis=0, keepdims=True), axis=1, keepdims=True)
    inverse_rms = lax.rsqrt(squares / (C * LANES) + 1e-06)
    normed = (x * inverse_rms * gain_ref[...]).astype(jnp.bfloat16)
    rows[r, z] = normed

    pl.semaphore_wait(barrier, len(peers) + 1)

    def row_copy(rr, zz, send_sem, zp, rp):
        return pltpu.make_async_remote_copy(
            src_ref=rows.at[rr, zz],
            dst_ref=rows.at[rr, zz],
            send_sem=send_sem,
            recv_sem=ag_recv.at[rr, zz],
            device_id={"expert": zp, "replica": rp},
            device_id_type=MESH,
        )

    for i, zp, rp in reversed(peers):
        row_copy(r, z, ag_send.at[i], zp, rp).start()
    row_copy(r, z, ag_send.at[len(peers)], z, partner).start()

    def spread(rr, zz):
        at = pl.multiple_of((rr * Z + zz) * C, C)
        flat[pl.ds(at, C), :] = rows[rr, zz].astype(jnp.float32)

    small[2].wait()
    small[3].wait()
    E = router_ref.shape[0]
    xs[...] = normed.astype(jnp.float32)
    logit_sums = jnp.zeros((E, LANES), jnp.float32)
    for c in range(C):
        logit_sums += (
            router_ref[:, pl.ds(c * LANES, LANES)].astype(jnp.float32) * xs[pl.ds(c, 1), :]
        )
    logits = jnp.broadcast_to(jnp.sum(logit_sums, axis=1, keepdims=True), (E, LANES))
    expert_ids = lax.broadcasted_iota(jnp.int32, (E, LANES), 0)
    members = jnp.zeros((E, LANES), jnp.float32)
    for t in range(routes_ref.shape[0]):
        members += (expert_ids == routes_ref[t, r]).astype(jnp.float32)
    chosen = members / (1.0 + jnp.exp(-logits))
    wts[...] = ROUTE_SCALE * chosen / jnp.sum(chosen, axis=0, keepdims=True)

    spread(r, z)
    for i, zp, rp in peers:
        row_copy(rp, zp, ag_send.at[i], zp, rp).wait_recv()
        row_copy(rp, zp, ag_pass.at[i], z, partner).start()
        spread(rp, zp)
    for i, zp, rp in [(len(peers), z, r)] + peers:
        other = rp + partner - r
        row_copy(other, zp, ag_send.at[i], z, partner).wait_recv()
        spread(other, zp)
    for c in range(C):
        lhs[:, pl.ds(c * LANES, LANES)] = flat[pl.ds(c, M, stride=C), :].astype(jnp.bfloat16)

    weights[0].wait()
    weights[1].wait()
    gate_up = jnp.dot(lhs[...], wgu[...], preferred_element_type=jnp.float32)
    gate_act, up_act = gate_up[:, :F], gate_up[:, F:]
    hidden = (gate_act / (1.0 + jnp.exp(-gate_act)) * up_act).astype(jnp.bfloat16)
    weights[2].wait()
    step = 4
    for n in range(C // step):
        piece = jnp.dot(
            hidden,
            wd[:, pl.ds(n * step * LANES, step * LANES)],
            preferred_element_type=jnp.float32,
        )
        for j in range(step):
            part[pl.ds(n * step + j, M, stride=C), :] = piece[:, j * LANES : (j + 1) * LANES]

    span = Z * C
    half = R // 2

    def pair_copy(k):
        return pltpu.make_async_remote_copy(
            src_ref=psnd.at[k],
            dst_ref=pgot.at[k],
            send_sem=rs_psend.at[k],
            recv_sem=rs_precv.at[k],
            device_id={"replica": partner},
            device_id_type=MESH,
        )

    mine_k = lax.div(r, 2)
    order = [lax.div(flip(r, 2 * b), 2) for b in reversed(range(half))]
    for k in order:
        at = pl.multiple_of((2 * k + 1 - core) * span, span)
        psnd[k] = part[pl.ds(at, span), :].astype(jnp.bfloat16)
        pair_copy(k).start()

    def sum_copy(i, zp, rp, own):
        kp = lax.div(rp, 2)
        slot = (mine_k, z) if own else (kp, zp)
        return pltpu.make_async_remote_copy(
            src_ref=snd.at[kp, zp],
            dst_ref=got.at[slot[0], slot[1]],
            send_sem=rs_send.at[i],
            recv_sem=rs_recv.at[slot[0], slot[1]],
            device_id={"expert": zp, "replica": rp},
            device_id_type=MESH,
        )

    for b in reversed(range(half)):
        k = order[half - 1 - b]
        pair_copy(k).wait_recv()
        at = pl.multiple_of((2 * k + core) * span, span)
        acc[...] = part[pl.ds(at, span), :] + pgot[k].astype(jnp.float32)
        for (i, zp, rp), (_, bb) in reversed(list(zip(peers, pairs))):
            if bb == 2 * b:
                snd[k, zp] = acc[pl.ds(pl.multiple_of(zp * C, C), C), :].astype(jnp.bfloat16)
                sum_copy(i, zp, rp, True).start()
    total = acc[pl.ds(pl.multiple_of(z * C, C), C), :] * wts[pl.ds(z, 1), :]
    for i, zp, rp in peers:
        sum_copy(i, zp, rp, False).wait_recv()
        total += got[lax.div(rp, 2), zp].astype(jnp.float32) * wts[pl.ds(zp, 1), :]

    for c in range(C):
        lane = pl.ds(c * LANES, LANES)
        out_ref[:, lane] = (
            x_ref[:, lane].astype(jnp.float32) + total[c : c + 1, :]
        ).astype(jnp.bfloat16)

    for i, zp, rp in peers:
        row_copy(r, z, ag_send.at[i], zp, rp).wait_send()
        row_copy(rp, zp, ag_pass.at[i], z, partner).wait_send()
        sum_copy(i, zp, rp, True).wait_send()
    row_copy(r, z, ag_send.at[len(peers)], z, partner).wait_send()
    for k in order:
        pair_copy(k).wait_send()


def solution(mesh):
    Z, R = mesh.shape["expert"], mesh.shape["replica"]

    def on_device(beam_rows, norm_gain, router, gate_proj, up_proj, down_proj, routes):
        D = beam_rows.shape[1]
        F = gate_proj.shape[2]
        C = D // LANES
        M = Z * R
        E = router.shape[1]
        vmem = pl.BlockSpec(memory_space=pltpu.VMEM)
        anywhere = pl.BlockSpec(memory_space=pl.ANY)
        dma = pltpu.SemaphoreType.DMA
        return pl.pallas_call(
            functools.partial(moe_kernel, Z, R),
            out_shape=jax.ShapeDtypeStruct(beam_rows.shape, jnp.bfloat16),
            in_specs=[anywhere] * 7,
            out_specs=vmem,
            scratch_shapes=[
                pltpu.VMEM(beam_rows.shape, beam_rows.dtype),
                pltpu.VMEM((C, LANES), jnp.float32),
                pltpu.VMEM((E, D), router.dtype),
                pltpu.SMEM(routes.shape[::-1], jnp.int32),
                pltpu.VMEM((D, 2 * F), jnp.bfloat16),
                pltpu.VMEM((F, D), jnp.bfloat16),
                pltpu.VMEM((C, LANES), jnp.float32),
                pltpu.VMEM((R, Z, C, LANES), jnp.bfloat16),
                pltpu.VMEM((M * C, LANES), jnp.float32),
                pltpu.VMEM((M, D), jnp.bfloat16),
                pltpu.VMEM((M * C, LANES), jnp.float32),
                pltpu.VMEM((R // 2, Z * C, LANES), jnp.bfloat16),
                pltpu.VMEM((R // 2, Z * C, LANES), jnp.bfloat16),
                pltpu.VMEM((Z * C, LANES), jnp.float32),
                pltpu.VMEM((R // 2, Z, C, LANES), jnp.bfloat16),
                pltpu.VMEM((R // 2, Z, C, LANES), jnp.bfloat16),
                pltpu.VMEM((E, LANES), jnp.float32),
                dma((7,)),
                dma((M // 2,)),
                dma((M // 2,)),
                dma((R, Z)),
                dma((R // 2,)),
                dma((R // 2,)),
                dma((M // 2,)),
                dma((R // 2, Z)),
            ],
            compiler_params=pltpu.CompilerParams(
                collective_id=0, has_side_effects=True, vmem_limit_bytes=VMEM_BYTES
            ),
        )(
            beam_rows,
            norm_gain.reshape(C, LANES),
            router.T,
            routes.T,
            gate_proj,
            up_proj,
            down_proj,
        )

    placed = (
        P(("groups", "expert", "replica"), None),
        P(),
        P(),
        P("expert", None, "replica"),
        P("expert", None, "replica"),
        P("expert", "replica", None),
        P(("groups", "expert"), None),
    )
    return jax.shard_map(
        on_device,
        mesh=mesh,
        in_specs=placed,
        out_specs=P(("groups", "expert", "replica"), None),
        check_vma=False,
    )
```

```python
import functools

import jax
import jax.numpy as jnp
from jax import lax
from jax.experimental import pallas as pl
from jax.experimental.pallas import tpu as pltpu
from jax.sharding import PartitionSpec as P

ROUTE_SCALE = 2.5
LANES = 128
VMEM_BYTES = 63 * 2**20


def moe_kernel(
    Z,
    R,
    x_hbm,
    gain_hbm,
    router_hbm,
    routes_hbm,
    gate_ref,
    up_ref,
    down_ref,
    out_ref,
    x_ref,
    gain_ref,
    router_ref,
    routes_ref,
    wgu,
    wd,
    xs,
    rows,
    flat,
    lhs,
    part,
    snd,
    got,
    wts,
    w_sem,
    ag_send,
    ag_recv,
    share_send,
    share_recv,
    rs_send,
    rs_recv,
):
    C = xs.shape[0]
    F = down_ref.shape[1]
    half = R // 2
    M = Z * half
    z = lax.axis_index("expert")
    r = lax.axis_index("replica")
    core = lax.rem(r, 2)
    partner = r + 1 - 2 * core
    mine = lax.div(r, 2)
    MESH = pl.DeviceIdType.MESH

    def flip(value, mask):
        bit = 1
        while bit <= mask:
            if mask & bit:
                value = value + bit - 2 * bit * lax.rem(lax.div(value, bit), 2)
            bit *= 2
        return value

    pairs = [(a, 2 * b) for a in range(Z) for b in range(R // 2) if a or b]
    pairs.sort(key=lambda p: p[0] + bin(p[1]).count("1"))
    peers = [(i, flip(z, a), flip(r, b)) for i, (a, b) in enumerate(pairs)]

    small = [
        pltpu.make_async_copy(x_hbm, x_ref, w_sem.at[3]),
        pltpu.make_async_copy(gain_hbm, gain_ref, w_sem.at[4]),
        pltpu.make_async_copy(router_hbm, router_ref, w_sem.at[5]),
        pltpu.make_async_copy(routes_hbm, routes_ref, w_sem.at[6]),
    ]
    for copy in small:
        copy.start()

    barrier = pltpu.get_barrier_semaphore()
    pl.semaphore_signal(barrier, inc=1, device_id={"replica": partner}, device_id_type=MESH)
    for _, zp, rp in peers:
        pl.semaphore_signal(
            barrier, inc=1, device_id={"expert": zp, "replica": rp}, device_id_type=MESH
        )

    weights = [
        pltpu.make_async_copy(gate_ref.at[0], wgu.at[:, pl.ds(0, F)], w_sem.at[0]),
        pltpu.make_async_copy(up_ref.at[0], wgu.at[:, pl.ds(F, F)], w_sem.at[1]),
        pltpu.make_async_copy(down_ref.at[0], wd.at[pl.ds(0, F), :], w_sem.at[2]),
    ]
    for copy in weights:
        copy.start()

    small[0].wait()
    small[1].wait()
    for c in range(C):
        xs[pl.ds(c, 1), :] = x_ref[:, pl.ds(c * LANES, LANES)].astype(jnp.float32)
    x = xs[...]
    squares = jnp.sum(jnp.sum(x * x, axis=0, keepdims=True), axis=1, keepdims=True)
    inverse_rms = lax.rsqrt(squares / (C * LANES) + 1e-06)
    normed = (x * inverse_rms * gain_ref[...]).astype(jnp.bfloat16)
    rows[mine, z] = normed

    pl.semaphore_wait(barrier, len(peers) + 1)

    def row_copy(k, zz, i, zp, rp):
        return pltpu.make_async_remote_copy(
            src_ref=rows.at[k, zz],
            dst_ref=rows.at[k, zz],
            send_sem=ag_send.at[i],
            recv_sem=ag_recv.at[k, zz],
            device_id={"expert": zp, "replica": rp},
            device_id_type=MESH,
        )

    for i, zp, rp in reversed(peers):
        row_copy(mine, z, i, zp, rp).start()

    def share(j, src, dst):
        return pltpu.make_async_remote_copy(
            src_ref=src,
            dst_ref=dst,
            send_sem=share_send.at[j],
            recv_sem=share_recv.at[j],
            device_id={"replica": partner},
            device_id_type=MESH,
        )

    shared = [
        share(0, gate_ref.at[0], wgu.at[:, pl.ds(2 * F, F)]),
        share(1, up_ref.at[0], wgu.at[:, pl.ds(3 * F, F)]),
        share(2, down_ref.at[0], wd.at[pl.ds(F, F), :]),
    ]
    for copy in shared:
        copy.start()

    def spread(k, zz):
        at = pl.multiple_of((k * Z + zz) * C, C)
        flat[pl.ds(at, C), :] = rows[k, zz].astype(jnp.float32)

    small[2].wait()
    small[3].wait()
    E = router_ref.shape[0]
    xs[...] = normed.astype(jnp.float32)
    logit_sums = jnp.zeros((E, LANES), jnp.float32)
    for c in range(C):
        logit_sums += (
            router_ref[:, pl.ds(c * LANES, LANES)].astype(jnp.float32) * xs[pl.ds(c, 1), :]
        )
    logits = jnp.broadcast_to(jnp.sum(logit_sums, axis=1, keepdims=True), (E, LANES))
    expert_ids = lax.broadcasted_iota(jnp.int32, (E, LANES), 0)
    members = jnp.zeros((E, LANES), jnp.float32)
    for t in range(routes_ref.shape[0]):
        members += (expert_ids == routes_ref[t, r]).astype(jnp.float32)
    chosen = members / (1.0 + jnp.exp(-logits))
    wts[...] = ROUTE_SCALE * chosen / jnp.sum(chosen, axis=0, keepdims=True)

    spread(mine, z)
    for i, zp, rp in peers:
        kp = lax.div(rp, 2)
        row_copy(kp, zp, i, zp, rp).wait_recv()
        spread(kp, zp)
    for c in range(C):
        lhs[:, pl.ds(c * LANES, LANES)] = flat[pl.ds(c, M, stride=C), :].astype(jnp.bfloat16)

    def hidden_of(at):
        gate_up = jnp.dot(
            lhs[...], wgu[:, pl.ds(at, 2 * F)], preferred_element_type=jnp.float32
        )
        gate_act, up_act = gate_up[:, :F], gate_up[:, F:]
        return (gate_act / (1.0 + jnp.exp(-gate_act)) * up_act).astype(jnp.bfloat16)

    weights[0].wait()
    weights[1].wait()
    own_hidden = hidden_of(0)
    shared[0].wait_recv()
    shared[1].wait_recv()
    hidden = jnp.concatenate([own_hidden, hidden_of(2 * F)], axis=1)
    weights[2].wait()
    shared[2].wait_recv()
    step = 4
    for n in range(C // step):
        piece = jnp.dot(
            hidden,
            wd[:, pl.ds(n * step * LANES, step * LANES)],
            preferred_element_type=jnp.float32,
        )
        for j in range(step):
            part[pl.ds(n * step + j, M, stride=C), :] = piece[:, j * LANES : (j + 1) * LANES]

    def sum_copy(i, zp, rp, own):
        kp = lax.div(rp, 2)
        slot = (mine, z) if own else (kp, zp)
        return pltpu.make_async_remote_copy(
            src_ref=snd.at[kp, zp],
            dst_ref=got.at[slot[0], slot[1]],
            send_sem=rs_send.at[i],
            recv_sem=rs_recv.at[slot[0], slot[1]],
            device_id={"expert": zp, "replica": rp},
            device_id_type=MESH,
        )

    def sums(k, zz):
        return part[pl.ds(pl.multiple_of((k * Z + zz) * C, C), C), :]

    for i, zp, rp in reversed(peers):
        kp = lax.div(rp, 2)
        snd[kp, zp] = sums(kp, zp).astype(jnp.bfloat16)
        sum_copy(i, zp, rp, True).start()
    total = sums(mine, z) * wts[pl.ds(z, 1), :]
    for i, zp, rp in peers:
        sum_copy(i, zp, rp, False).wait_recv()
        total += got[lax.div(rp, 2), zp].astype(jnp.float32) * wts[pl.ds(zp, 1), :]

    for c in range(C):
        lane = pl.ds(c * LANES, LANES)
        out_ref[:, lane] = (
            x_ref[:, lane].astype(jnp.float32) + total[c : c + 1, :]
        ).astype(jnp.bfloat16)

    for i, zp, rp in peers:
        row_copy(mine, z, i, zp, rp).wait_send()
        sum_copy(i, zp, rp, True).wait_send()
    for copy in shared:
        copy.wait_send()


def solution(mesh):
    Z, R = mesh.shape["expert"], mesh.shape["replica"]

    def on_device(beam_rows, norm_gain, router, gate_proj, up_proj, down_proj, routes):
        D = beam_rows.shape[1]
        F = gate_proj.shape[2]
        C = D // LANES
        M = Z * R // 2
        E = router.shape[1]
        vmem = pl.BlockSpec(memory_space=pltpu.VMEM)
        anywhere = pl.BlockSpec(memory_space=pl.ANY)
        dma = pltpu.SemaphoreType.DMA
        return pl.pallas_call(
            functools.partial(moe_kernel, Z, R),
            out_shape=jax.ShapeDtypeStruct(beam_rows.shape, jnp.bfloat16),
            in_specs=[anywhere] * 7,
            out_specs=vmem,
            scratch_shapes=[
                pltpu.VMEM(beam_rows.shape, beam_rows.dtype),
                pltpu.VMEM((C, LANES), jnp.float32),
                pltpu.VMEM((E, D), router.dtype),
                pltpu.SMEM(routes.shape[::-1], jnp.int32),
                pltpu.VMEM((D, 4 * F), jnp.bfloat16),
                pltpu.VMEM((2 * F, D), jnp.bfloat16),
                pltpu.VMEM((C, LANES), jnp.float32),
                pltpu.VMEM((R // 2, Z, C, LANES), jnp.bfloat16),
                pltpu.VMEM((M * C, LANES), jnp.float32),
                pltpu.VMEM((M, D), jnp.bfloat16),
                pltpu.VMEM((M * C, LANES), jnp.float32),
                pltpu.VMEM((R // 2, Z, C, LANES), jnp.bfloat16),
                pltpu.VMEM((R // 2, Z, C, LANES), jnp.bfloat16),
                pltpu.VMEM((E, LANES), jnp.float32),
                dma((7,)),
                dma((M,)),
                dma((R // 2, Z)),
                dma((3,)),
                dma((3,)),
                dma((M,)),
                dma((R // 2, Z)),
            ],
            compiler_params=pltpu.CompilerParams(
                collective_id=0, has_side_effects=True, vmem_limit_bytes=VMEM_BYTES
            ),
        )(
            beam_rows,
            norm_gain.reshape(C, LANES),
            router.T,
            routes.T,
            gate_proj,
            up_proj,
            down_proj,
        )

    placed = (
        P(("groups", "expert", "replica"), None),
        P(),
        P(),
        P("expert", None, "replica"),
        P("expert", None, "replica"),
        P("expert", "replica", None),
        P(("groups", "expert"), None),
    )
    return jax.shard_map(
        on_device,
        mesh=mesh,
        in_specs=placed,
        out_specs=P(("groups", "expert", "replica"), None),
        check_vma=False,
    )
```

```python
import functools

import jax
import jax.numpy as jnp
from jax import lax
from jax.experimental import pallas as pl
from jax.experimental.pallas import tpu as pltpu
from jax.sharding import PartitionSpec as P

ROUTE_SCALE = 2.5
LANES = 128
VMEM_BYTES = 63 * 2**20


def moe_kernel(
    Z,
    R,
    x_hbm,
    gain_hbm,
    router_hbm,
    routes_hbm,
    gate_ref,
    up_ref,
    down_ref,
    out_ref,
    x_ref,
    gain_ref,
    router_ref,
    routes_ref,
    wgu,
    wd,
    xs,
    rows,
    flat,
    lhs,
    part,
    snd,
    got,
    wts,
    w_sem,
    ag_send,
    ag_recv,
    share_send,
    share_recv,
    rs_send,
    rs_recv,
):
    C = xs.shape[0]
    F = down_ref.shape[1]
    half = R // 2
    M = Z * half
    z = lax.axis_index("expert")
    r = lax.axis_index("replica")
    core = lax.rem(r, 2)
    partner = r + 1 - 2 * core
    mine = lax.div(r, 2)
    MESH = pl.DeviceIdType.MESH

    def flip(value, mask):
        bit = 1
        while bit <= mask:
            if mask & bit:
                value = value + bit - 2 * bit * lax.rem(lax.div(value, bit), 2)
            bit *= 2
        return value

    pairs = [(a, 2 * b) for a in range(Z) for b in range(R // 2) if a or b]
    pairs.sort(key=lambda p: p[0] + bin(p[1]).count("1"))
    peers = [(i, flip(z, a), flip(r, b)) for i, (a, b) in enumerate(pairs)]

    small = [
        pltpu.make_async_copy(x_hbm, x_ref, w_sem.at[3]),
        pltpu.make_async_copy(gain_hbm, gain_ref, w_sem.at[4]),
        pltpu.make_async_copy(router_hbm, router_ref, w_sem.at[5]),
        pltpu.make_async_copy(routes_hbm, routes_ref, w_sem.at[6]),
    ]
    for copy in small:
        copy.start()

    barrier = pltpu.get_barrier_semaphore()
    pl.semaphore_signal(barrier, inc=1, device_id={"replica": partner}, device_id_type=MESH)
    for _, zp, rp in peers:
        pl.semaphore_signal(
            barrier, inc=1, device_id={"expert": zp, "replica": rp}, device_id_type=MESH
        )

    weights = [
        pltpu.make_async_copy(gate_ref.at[0], wgu.at[:, pl.ds(0, F)], w_sem.at[0]),
        pltpu.make_async_copy(up_ref.at[0], wgu.at[:, pl.ds(F, F)], w_sem.at[1]),
        pltpu.make_async_copy(down_ref.at[0], wd.at[pl.ds(0, F), :], w_sem.at[2]),
    ]
    for copy in weights:
        copy.start()

    small[0].wait()
    small[1].wait()
    for c in range(C):
        xs[pl.ds(c, 1), :] = x_ref[:, pl.ds(c * LANES, LANES)].astype(jnp.float32)
    x = xs[...]
    squares = jnp.sum(jnp.sum(x * x, axis=0, keepdims=True), axis=1, keepdims=True)
    inverse_rms = lax.rsqrt(squares / (C * LANES) + 1e-06)
    normed = (x * inverse_rms * gain_ref[...]).astype(jnp.bfloat16)
    rows[mine, z] = normed

    pl.semaphore_wait(barrier, len(peers) + 1)

    def row_copy(k, zz, i, zp, rp):
        return pltpu.make_async_remote_copy(
            src_ref=rows.at[k, zz],
            dst_ref=rows.at[k, zz],
            send_sem=ag_send.at[i],
            recv_sem=ag_recv.at[k, zz],
            device_id={"expert": zp, "replica": rp},
            device_id_type=MESH,
        )

    for i, zp, rp in reversed(peers):
        row_copy(mine, z, i, zp, rp).start()

    def share(j, src, dst):
        return pltpu.make_async_remote_copy(
            src_ref=src,
            dst_ref=dst,
            send_sem=share_send.at[j],
            recv_sem=share_recv.at[j],
            device_id={"replica": partner},
            device_id_type=MESH,
        )

    shared = [
        share(0, gate_ref.at[0], wgu.at[:, pl.ds(2 * F, F)]),
        share(1, up_ref.at[0], wgu.at[:, pl.ds(3 * F, F)]),
        share(2, down_ref.at[0], wd.at[pl.ds(F, F), :]),
    ]
    for copy in shared:
        copy.start()

    def spread(k, zz):
        at = pl.multiple_of((k * Z + zz) * C, C)
        flat[pl.ds(at, C), :] = rows[k, zz].astype(jnp.float32)

    small[2].wait()
    small[3].wait()
    E = router_ref.shape[0]
    xs[...] = normed.astype(jnp.float32)
    logit_sums = jnp.zeros((E, LANES), jnp.float32)
    for c in range(C):
        logit_sums += (
            router_ref[:, pl.ds(c * LANES, LANES)].astype(jnp.float32) * xs[pl.ds(c, 1), :]
        )
    logits = jnp.broadcast_to(jnp.sum(logit_sums, axis=1, keepdims=True), (E, LANES))
    expert_ids = lax.broadcasted_iota(jnp.int32, (E, LANES), 0)
    members = jnp.zeros((E, LANES), jnp.float32)
    for t in range(routes_ref.shape[0]):
        members += (expert_ids == routes_ref[t, r]).astype(jnp.float32)
    chosen = members / (1.0 + jnp.exp(-logits))
    wts[...] = ROUTE_SCALE * chosen / jnp.sum(chosen, axis=0, keepdims=True)

    spread(mine, z)
    for i, zp, rp in peers:
        kp = lax.div(rp, 2)
        row_copy(kp, zp, i, zp, rp).wait_recv()
        spread(kp, zp)
    for c in range(C):
        lhs[:, pl.ds(c * LANES, LANES)] = flat[pl.ds(c, M, stride=C), :].astype(jnp.bfloat16)

    for copy in weights:
        copy.wait()
    shared[0].wait_recv()
    shared[1].wait_recv()
    acts = jnp.dot(lhs[...], wgu[...], preferred_element_type=jnp.float32)
    gates = jnp.concatenate([acts[:, :F], acts[:, 2 * F : 3 * F]], axis=1)
    ups = jnp.concatenate([acts[:, F : 2 * F], acts[:, 3 * F :]], axis=1)
    hidden = (gates / (1.0 + jnp.exp(-gates)) * ups).astype(jnp.bfloat16)
    shared[2].wait_recv()
    step = 4
    for n in range(C // step):
        piece = jnp.dot(
            hidden,
            wd[:, pl.ds(n * step * LANES, step * LANES)],
            preferred_element_type=jnp.float32,
        )
        for j in range(step):
            part[pl.ds(n * step + j, M, stride=C), :] = piece[:, j * LANES : (j + 1) * LANES]

    def sum_copy(i, zp, rp, own):
        kp = lax.div(rp, 2)
        slot = (mine, z) if own else (kp, zp)
        return pltpu.make_async_remote_copy(
            src_ref=snd.at[kp, zp],
            dst_ref=got.at[slot[0], slot[1]],
            send_sem=rs_send.at[i],
            recv_sem=rs_recv.at[slot[0], slot[1]],
            device_id={"expert": zp, "replica": rp},
            device_id_type=MESH,
        )

    def sums(k, zz):
        return part[pl.ds(pl.multiple_of((k * Z + zz) * C, C), C), :]

    for i, zp, rp in reversed(peers):
        kp = lax.div(rp, 2)
        snd[kp, zp] = sums(kp, zp).astype(jnp.bfloat16)
        sum_copy(i, zp, rp, True).start()
    for i, zp, rp in peers:
        row_copy(mine, z, i, zp, rp).wait_send()
        sum_copy(i, zp, rp, True).wait_send()
    for copy in shared:
        copy.wait_send()
    total = sums(mine, z) * wts[pl.ds(z, 1), :]
    for i, zp, rp in peers:
        sum_copy(i, zp, rp, False).wait_recv()
        total += got[lax.div(rp, 2), zp].astype(jnp.float32) * wts[pl.ds(zp, 1), :]

    xs[...] = x + total
    for c in range(C):
        out_ref[:, pl.ds(c * LANES, LANES)] = xs[pl.ds(c, 1), :].astype(jnp.bfloat16)


def solution(mesh):
    Z, R = mesh.shape["expert"], mesh.shape["replica"]

    def on_device(beam_rows, norm_gain, router, gate_proj, up_proj, down_proj, routes):
        D = beam_rows.shape[1]
        F = gate_proj.shape[2]
        C = D // LANES
        M = Z * R // 2
        E = router.shape[1]
        vmem = pl.BlockSpec(memory_space=pltpu.VMEM)
        anywhere = pl.BlockSpec(memory_space=pl.ANY)
        dma = pltpu.SemaphoreType.DMA
        return pl.pallas_call(
            functools.partial(moe_kernel, Z, R),
            out_shape=jax.ShapeDtypeStruct(beam_rows.shape, jnp.bfloat16),
            in_specs=[anywhere] * 7,
            out_specs=vmem,
            scratch_shapes=[
                pltpu.VMEM(beam_rows.shape, beam_rows.dtype),
                pltpu.VMEM((C, LANES), jnp.float32),
                pltpu.VMEM((E, D), router.dtype),
                pltpu.SMEM(routes.shape[::-1], jnp.int32),
                pltpu.VMEM((D, 4 * F), jnp.bfloat16),
                pltpu.VMEM((2 * F, D), jnp.bfloat16),
                pltpu.VMEM((C, LANES), jnp.float32),
                pltpu.VMEM((R // 2, Z, C, LANES), jnp.bfloat16),
                pltpu.VMEM((M * C, LANES), jnp.float32),
                pltpu.VMEM((M, D), jnp.bfloat16),
                pltpu.VMEM((M * C, LANES), jnp.float32),
                pltpu.VMEM((R // 2, Z, C, LANES), jnp.bfloat16),
                pltpu.VMEM((R // 2, Z, C, LANES), jnp.bfloat16),
                pltpu.VMEM((E, LANES), jnp.float32),
                dma((7,)),
                dma((M,)),
                dma((R // 2, Z)),
                dma((3,)),
                dma((3,)),
                dma((M,)),
                dma((R // 2, Z)),
            ],
            compiler_params=pltpu.CompilerParams(
                collective_id=0, has_side_effects=True, vmem_limit_bytes=VMEM_BYTES
            ),
        )(
            beam_rows,
            norm_gain.reshape(C, LANES),
            router.T,
            routes.T,
            gate_proj,
            up_proj,
            down_proj,
        )

    placed = (
        P(("groups", "expert", "replica"), None),
        P(),
        P(),
        P("expert", None, "replica"),
        P("expert", None, "replica"),
        P("expert", "replica", None),
        P(("groups", "expert"), None),
    )
    return jax.shard_map(
        on_device,
        mesh=mesh,
        in_specs=placed,
        out_specs=P(("groups", "expert", "replica"), None),
        check_vma=False,
    )
```
